32 devices in a mesh: slab: 16 (over z, y, x), kv: 2 (over core).
Axes of the slice: x: 2, y: 2, z: 4, core: 2. Of those that a mesh axis runs over, the one named last changes fastest.
Arguments:
- queries: bfloat16 [16384, 512], P('slab'), may hold values from -6 to 6
- grad_out: bfloat16 [16384, 512], P('slab'), may hold values from -6 to 6
- attn_out: bfloat16 [16384, 512], P('slab'), may hold values from -6 to 6
- row_lse: float32 [16384], P('slab'), may hold values from 5.5 to 7.5
- keys: bfloat16 [2, 2048, 512], P('kv', 'slab'), may hold values from -6 to 6
- values: bfloat16 [2, 2048, 512], P('kv', 'slab'), may hold values from -6 to 6
Outputs:
- grad_queries: bfloat16 [16384, 512], P('slab', 'kv')
- grad_keys: bfloat16 [2, 2048, 512], P('kv', 'slab')
- grad_values: bfloat16 [2, 2048, 512], P('kv', 'slab')
The draws below stay inside these ranges and needn't reach their ends.
All inputs are finite; a program needn't handle non-finite values.
Results may differ from the reference program's by a relative error of at most 0.005.
Values may be sent and summed in bfloat16 or wider, within the bound.
A program may use at most 128 MiB of HBM per device.

```python
import jax
import jax.numpy as jnp
from jax import lax

C = 512
TOK_DEV = 1024
KPANEL = 2048
TOKENS = 16384
N_SLAB = 16
N_KV = 2


def shard_levels(own_key, dims, shards, low, high):
    loudness = 1.0
    for axis_at, shards_of in shards:
        heights = jax.random.uniform(jax.random.fold_in(jax.random.fold_in(own_key, 6), axis_at), (shards_of,), jnp.float32, low / len(shards), high / len(shards))
        loudness = loudness * jnp.repeat(jnp.exp(heights), dims[axis_at] // shards_of).reshape((-1,) + (1,) * (len(dims) - 1 - axis_at))
    return loudness


def bell_draw(key, extent, scale, limit, shards=(), kind=jnp.bfloat16):
    result = jax.random.normal(key, extent, jnp.float32) * scale
    if len(shards) > 0:
        result = shard_levels(key, extent, shards, -0.22, 0.18) * result
    return jnp.clip(result, min=-limit, max=limit).astype(kind)


def setup_inputs(seed: int = 0) -> dict:
    key_of = jax.random.split(jax.random.key(seed), 7)
    queries = bell_draw(key_of[0], (TOKENS, C), 1.0, 6.0, ((0, 16),))
    grad_out = bell_draw(key_of[1], (TOKENS, C), 1.0, 6.0, ((0, 16),))
    attn_out = bell_draw(key_of[2], (TOKENS, C), 1.0, 6.0, ((0, 16),))
    row_lse = jnp.clip(5.5 + 2.0 * jax.random.uniform(key_of[3], (TOKENS,), jnp.float32) ** shard_levels(key_of[3], (TOKENS,), ((0, 16),), -0.2, 0.2), 5.5, 7.5)
    keys = bell_draw(key_of[4], (N_KV, KPANEL, C), 1.0, 6.0, ((0, 2), (1, 16)))
    values = bell_draw(key_of[5], (N_KV, KPANEL, C), 1.0, 6.0, ((0, 2), (1, 16)))
    return {"queries": queries, "grad_out": grad_out, "attn_out": attn_out, "row_lse": row_lse, "keys": keys, "values": values}


def reference(queries, grad_out, attn_out, row_lse, keys, values):
    score_scale = C ** -0.5

    def one_block(carry, block_index):
        grad_keys_acc, grad_values_acc = carry
        start = (block_index * TOK_DEV).astype(jnp.int32)
        query_rows = lax.dynamic_slice_in_dim(queries, start, TOK_DEV, 0)
        grad_rows = lax.dynamic_slice_in_dim(grad_out, start, TOK_DEV, 0)
        out_rows = lax.dynamic_slice_in_dim(attn_out, start, TOK_DEV, 0)
        lse_rows = lax.dynamic_slice_in_dim(row_lse, start, TOK_DEV, 0)
        stats = jnp.sum(grad_rows.astype(jnp.float32) * out_rows.astype(jnp.float32), axis=1)
        grad_query = jnp.zeros((TOK_DEV, C), jnp.float32)
        for panel in range(N_KV):
            panel_keys = keys[panel]
            panel_values = values[panel]
            scores = jnp.dot(query_rows, panel_keys.T, preferred_element_type=jnp.float32) * score_scale
            probs = jnp.exp(scores - lse_rows[:, None])
            probs_low = probs.astype(jnp.bfloat16)
            dprobs = jnp.dot(grad_rows, panel_values.T, preferred_element_type=jnp.float32)
            dscores = (probs * (dprobs - stats[:, None])).astype(jnp.bfloat16)
            grad_query = grad_query + jnp.dot(dscores, panel_keys, preferred_element_type=jnp.float32) * score_scale
            key_term = jnp.dot(dscores.T, query_rows, preferred_element_type=jnp.float32) * score_scale
            value_term = jnp.dot(probs_low.T, grad_rows, preferred_element_type=jnp.float32)
            grad_keys_acc = grad_keys_acc.at[panel].add(key_term)
            grad_values_acc = grad_values_acc.at[panel].add(value_term)
        return (grad_keys_acc, grad_values_acc), grad_query.astype(jnp.bfloat16)

    empty = jnp.zeros((N_KV, KPANEL, C), jnp.float32)
    (grad_keys_sum, grad_values_sum), grad_blocks = lax.scan(one_block, (empty, empty), jnp.arange(N_SLAB, dtype=jnp.int32))
    grad_queries = grad_blocks.reshape(TOKENS, C)
    return grad_queries, grad_keys_sum.astype(jnp.bfloat16), grad_values_sum.astype(jnp.bfloat16)
```

```python
import functools
import math

import jax
import jax.numpy as jnp
from jax import lax
from jax.experimental import pallas as pl
from jax.experimental.pallas import tpu as pltpu
from jax.sharding import PartitionSpec as P

MESH = pl.DeviceIdType.MESH
F32 = jnp.float32
BF16 = jnp.bfloat16


def slab_layout(mesh):
    n_slab = mesh.shape["slab"]
    plain = ((n_slab, 1), (1, 1), (1, 1))
    try:
        coords = [tuple(d.coords) for d in mesh.devices[:, 0]]
    except (AttributeError, TypeError):
        return plain
    low = [min(c[p] for c in coords) for p in range(3)]
    coords = [tuple(c[p] - low[p] for p in range(3)) for c in coords]
    sizes = [max(c[p] for c in coords) + 1 for p in range(3)]
    if math.prod(sizes) != n_slab or len(set(coords)) != n_slab:
        return plain
    axes = []
    for p in range(3):
        unit = tuple(1 if q == p else 0 for q in range(3))
        axes.append((sizes[p], coords.index(unit) if sizes[p] > 1 else 1))
    for index, c in enumerate(coords):
        if any((index // axes[p][1]) % axes[p][0] != c[p] for p in range(3)):
            return plain
    (x, y, z) = axes
    return (z, y, x)


def kernel_body(
    layout, n_kv, scale,
    q_ref, do_ref, o_ref, lse_ref, k_ref, v_ref,
    dq_ref, dk_ref, dv_ref,
    kv, probs, dscores, acc, send_a, recv_a, send_b, recv_b, send_z, recv_z,
    dq_acc, dq_recv, rows,
    gz_s, gz_r, ga_s, ga_r, gb_s, gb_r, ra_s, ra_r, rb_s, rb_r, rz_s, rz_r, kv_s, kv_r,
):
    (nz, sz), (n_first, s_first), (n_second, s_second) = layout
    me = lax.axis_index("slab")
    core = lax.axis_index("kv")
    z = (me // sz) % nz
    first = (me // s_first) % n_first
    second = (me // s_second) % n_second
    na, nb = n_first, n_second
    if na == nb:
        odd = core % 2
        a = first + odd * (second - first)
        b = second + odd * (first - second)
        sa = s_first + odd * (s_second - s_first)
        sb = s_second + odd * (s_first - s_second)
    else:
        a, b, sa, sb = first, second, s_first, s_second
    kb = k_ref.shape[1]
    channels = k_ref.shape[2]
    tokens = q_ref.shape[0]
    col = nz * kb
    started = []

    def zp(d):
        return (z + d) % nz

    def ap(d):
        return (a + d) % na

    def bp(d):
        return (b + d) % nb

    def to_z(d):
        return (me + (zp(d) - z) * sz, core)

    def to_a(d):
        return (me + (ap(d) - a) * sa, core)

    def to_b(d):
        return (me + (bp(d) - b) * sb, core)

    def to_core(d):
        return (me, (core + d) % n_kv)

    def row(block):
        return pl.ds(pl.multiple_of(block * kb, kb), kb)

    def slot(rb, ra, rz):
        return row((bp(nb - rb) * na + ap(na - ra)) * nz + zp(nz - rz))

    def half(rb, rz):
        return row(bp(nb - rb) * nz + zp(nz - rz))

    def remote(src, dst, s, r, device):
        return pltpu.make_async_remote_copy(
            src_ref=src, dst_ref=dst, send_sem=s, recv_sem=r, device_id=device, device_id_type=MESH
        )

    def start(copy):
        copy.start()
        started.append(copy)

    peers = (
        [to_z(d) for d in range(1, nz)]
        + [to_a(d) for d in range(1, na)]
        + [to_b(d) for d in range(1, nb)]
        + [to_core(d) for d in range(1, n_kv)]
    )
    barrier = pltpu.get_barrier_semaphore()
    for peer in peers:
        pl.semaphore_signal(barrier, inc=1, device_id=peer, device_id_type=MESH)
    own = slot(0, 0, 0)
    kv[0, own, :] = k_ref[0]
    kv[1, own, :] = v_ref[0]
    pl.semaphore_wait(barrier, len(peers))

    def gather_z(d):
        s = kv.at[:, slot(0, 0, 0), :]
        return remote(s, s, gz_s.at[d - 1], gz_r.at[d - 1], to_z(d))

    def gather_a(d, rz):
        s = kv.at[:, slot(0, 0, rz), :]
        return remote(s, s, ga_s.at[d - 1, rz], ga_r.at[d - 1, rz], to_a(d))

    def gather_b(d, ra, rz):
        s = kv.at[:, slot(0, ra, rz), :]
        return remote(s, s, gb_s.at[d - 1, ra, rz], gb_r.at[d - 1, ra, rz], to_b(d))

    def arrived_z(d):
        s = kv.at[:, slot(0, 0, d), :]
        remote(s, s, gz_s.at[d - 1], gz_r.at[d - 1], to_z(d)).wait_recv()

    def arrived_a(d, rz):
        s = kv.at[:, slot(0, d, rz), :]
        remote(s, s, ga_s.at[d - 1, rz], ga_r.at[d - 1, rz], to_a(d)).wait_recv()

    def arrived_b(d, ra, rz):
        s = kv.at[:, slot(d, ra, rz), :]
        remote(s, s, gb_s.at[d - 1, ra, rz], gb_r.at[d - 1, ra, rz], to_b(d)).wait_recv()

    for d in range(1, nz):
        start(gather_z(d))
    for d in range(1, na):
        start(gather_a(d, 0))
    for d in range(1, nb):
        start(gather_b(d, 0, 0))

    qt = min(256, tokens)
    log2e = math.log2(math.e)

    @pl.loop(0, tokens // qt)
    def _(t):
        here = pl.ds(pl.multiple_of(t * qt, qt), qt)
        prod = do_ref[here, :].astype(F32) * o_ref[here, :].astype(F32)
        part = prod[:, :128]
        for lane in range(128, channels, 128):
            part = part + prod[:, lane : lane + 128]
        rows[1:2, here] = jnp.sum(part.T, axis=0, keepdims=True)
        rows[0:1, here] = lse_ref[:, here] * log2e

    for rz in range(1, nz):
        arrived_z(rz)
        for d in range(1, na):
            start(gather_a(d, rz))
        for d in range(1, nb):
            start(gather_b(d, 0, rz))

    kt = min(256, col)

    def column(rb, ra):
        top = pl.multiple_of((bp(nb - rb) * na + ap(na - ra)) * col, col)
        local = pl.multiple_of(bp(nb - rb) * col, col)

        @pl.loop(0, tokens // qt)
        def _(t):
            here = pl.ds(pl.multiple_of(t * qt, qt), qt)
            contract = (((1,), (1,)), ((), ()))
            span = pl.ds(top, col)
            s = lax.dot_general(kv[0, span, :], q_ref[here, :], contract, preferred_element_type=F32)
            p = jnp.exp2(s * (scale * log2e) - rows[0:1, here])
            dp = lax.dot_general(kv[1, span, :], do_ref[here, :], contract, preferred_element_type=F32)
            probs[:, here] = p.astype(BF16)
            dscores[span, here] = (p * (dp - rows[1:2, here])).astype(BF16)

        @pl.loop(0, col // kt)
        def _(t):
            off = t * kt
            span = pl.ds(pl.multiple_of(top + off, kt), kt)
            dk = jnp.dot(dscores[span, :], q_ref[...], preferred_element_type=F32)
            dv = jnp.dot(
                probs[pl.ds(pl.multiple_of(off, kt), kt), :], do_ref[...], preferred_element_type=F32
            )
            if ra == 0:
                there = pl.ds(pl.multiple_of(local + off, kt), kt)
                acc[0, there, :] = dk
                acc[1, there, :] = dv
            else:
                send_a[0, span, :] = dk.astype(BF16)
                send_a[1, span, :] = dv.astype(BF16)

    order_z = list(range(1, nz)) + [0]

    def reduce_a(ra, rb, rz):
        d = na - ra
        return remote(
            send_a.at[:, slot(rb, ra, rz), :], recv_a.at[d - 1, :, half(rb, rz), :],
            ra_s.at[d - 1, rb, rz], ra_r.at[d - 1, rb, rz], to_a(d),
        )

    def summed_a(d, rb, rz):
        here = half(rb, rz)
        dst = recv_a.at[d - 1, :, here, :]
        remote(dst, dst, ra_s.at[d - 1, rb, rz], ra_r.at[d - 1, rb, rz], to_a(d)).wait_recv()

    def reduce_b(rb, rz):
        d = nb - rb
        return remote(
            send_b.at[:, half(rb, rz), :], recv_b.at[d - 1, :, row(zp(nz - rz)), :],
            rb_s.at[d - 1, rz], rb_r.at[d - 1, rz], to_b(d),
        )

    def summed_b(d, rz):
        dst = recv_b.at[d - 1, :, row(zp(nz - rz)), :]
        remote(dst, dst, rb_s.at[d - 1, rz], rb_r.at[d - 1, rz], to_b(d)).wait_recv()

    def reduce_z(rz):
        d = nz - rz
        return remote(
            send_z.at[:, row(zp(d)), :], recv_z.at[d - 1], rz_s.at[d - 1], rz_r.at[d - 1], to_z(d)
        )

    column(0, 0)
    for rz in range(nz):
        for d in range(1, na):
            arrived_a(d, rz)
            for e in range(1, nb):
                start(gather_b(e, d, rz))
    for ra in range(1, na):
        column(0, ra)
        for rz in order_z:
            start(reduce_a(ra, 0, rz))
    for rb in range(1, nb):
        for rz in range(nz):
            arrived_b(rb, 0, rz)
        column(rb, 0)
    for rb in range(1, nb):
        for ra in range(1, na):
            for rz in range(nz):
                arrived_b(rb, ra, rz)
            column(rb, ra)
            for rz in order_z:
                start(reduce_a(ra, rb, rz))

    width = channels // n_kv

    @pl.loop(0, tokens // qt)
    def _(t):
        here = pl.ds(pl.multiple_of(t * qt, qt), qt)
        dq = lax.dot_general(
            dscores[:, here], kv[0], (((0,), (0,)), ((), ())), preferred_element_type=F32
        )
        for c in range(n_kv):
            dq_acc[c, here, :] = dq[:, c * width : (c + 1) * width]

    for d in range(1, n_kv):
        start(remote(
            dq_acc.at[(core + d) % n_kv], dq_recv.at[d - 1], kv_s.at[d - 1], kv_r.at[d - 1], to_core(d)
        ))

    def sum_a(rb, rz):
        here = half(rb, rz)
        total = acc[:, here, :]
        for d in range(1, na):
            summed_a(d, rb, rz)
            total = total + recv_a[d - 1, :, here, :].astype(F32)
        return total

    for rb in range(1, nb):
        for rz in order_z:
            send_b[:, half(rb, rz), :] = sum_a(rb, rz).astype(BF16)
            start(reduce_b(rb, rz))
    for rz in order_z:
        total = sum_a(0, rz)
        for d in range(1, nb):
            summed_b(d, rz)
            total = total + recv_b[d - 1, :, row(zp(nz - rz)), :].astype(F32)
        if rz != 0:
            send_z[:, row(zp(nz - rz)), :] = total.astype(BF16)
            start(reduce_z(rz))
        else:
            acc[:, half(0, 0), :] = total

    for d in range(1, n_kv):
        dst = dq_recv.at[d - 1]
        remote(dst, dst, kv_s.at[d - 1], kv_r.at[d - 1], to_core(d)).wait_recv()
    dq = dq_acc[core]
    for d in range(1, n_kv):
        dq = dq + dq_recv[d - 1]
    dq_ref[...] = (dq * scale).astype(BF16)

    total = acc[:, half(0, 0), :]
    for d in range(1, nz):
        dst = recv_z.at[d - 1]
        remote(dst, dst, rz_s.at[d - 1], rz_r.at[d - 1], to_z(d)).wait_recv()
        total = total + recv_z[d - 1].astype(F32)
    dk_ref[0] = (total[0] * scale).astype(BF16)
    dv_ref[0] = total[1].astype(BF16)
    for copy in started:
        copy.wait_send()


def solution(mesh):
    layout = slab_layout(mesh)
    n_kv = mesh.shape["kv"]
    (nz, _), (na, _), (nb, _) = layout

    def on_device(queries, grad_out, attn_out, row_lse, keys, values):
        tokens, channels = queries.shape
        kb = keys.shape[1]
        scale = channels ** (-0.5)
        col = nz * kb
        panel = na * nb * col
        width = channels // n_kv
        dma = pltpu.SemaphoreType.DMA

        def sems(*dims):
            dims = tuple(max(d, 1) for d in dims)
            return [dma(dims), dma(dims)]

        def buf(dtype, *dims):
            return pltpu.VMEM(tuple(max(d, 1) for d in dims), dtype)

        vmem = pl.BlockSpec(memory_space=pltpu.VMEM)
        return pl.pallas_call(
            functools.partial(kernel_body, layout, n_kv, scale),
            out_shape=(
                jax.ShapeDtypeStruct((tokens, width), BF16),
                jax.ShapeDtypeStruct(keys.shape, BF16),
                jax.ShapeDtypeStruct(values.shape, BF16),
            ),
            in_specs=[vmem] * 6,
            out_specs=(vmem,) * 3,
            scratch_shapes=[
                buf(BF16, 2, panel, channels),
                buf(BF16, col, tokens),
                buf(BF16, panel, tokens),
                buf(F32, 2, nb * col, channels),
                buf(BF16, 2, panel, channels),
                buf(BF16, na - 1, 2, nb * col, channels),
                buf(BF16, 2, nb * col, channels),
                buf(BF16, nb - 1, 2, col, channels),
                buf(BF16, 2, col, channels),
                buf(BF16, nz - 1, 2, kb, channels),
                buf(F32, n_kv, tokens, width),
                buf(F32, n_kv - 1, tokens, width),
                buf(F32, 8, tokens),
                *sems(nz - 1),
                *sems(na - 1, nz),
                *sems(nb - 1, na, nz),
                *sems(na - 1, nb, nz),
                *sems(nb - 1, nz),
                *sems(nz - 1),
                *sems(n_kv - 1),
            ],
            compiler_params=pltpu.CompilerParams(
                collective_id=0, has_side_effects=True, vmem_limit_bytes=56 * 1024 * 1024
            ),
            name="attention_backward",
        )(queries, grad_out, attn_out, row_lse.reshape(1, tokens), keys, values)

    placed = (
        P("slab", None),
        P("slab", None),
        P("slab", None),
        P("slab"),
        P("kv", "slab", None),
        P("kv", "slab", None),
    )
    return jax.shard_map(
        on_device,
        mesh=mesh,
        in_specs=placed,
        out_specs=(P("slab", "kv"), P("kv", "slab", None), P("kv", "slab", None)),
        check_vma=False,
    )
```

```python
import functools
import math

import jax
import jax.numpy as jnp
from jax import lax
from jax.experimental import pallas as pl
from jax.experimental.pallas import tpu as pltpu
from jax.sharding import PartitionSpec as P

MESH = pl.DeviceIdType.MESH
F32 = jnp.float32
BF16 = jnp.bfloat16


def slab_layout(mesh):
    n_slab = mesh.shape["slab"]
    plain = ((n_slab, 1), (1, 1), (1, 1))
    try:
        coords = [tuple(d.coords) for d in mesh.devices[:, 0]]
    except (AttributeError, TypeError):
        return plain
    low = [min(c[p] for c in coords) for p in range(3)]
    coords = [tuple(c[p] - low[p] for p in range(3)) for c in coords]
    sizes = [max(c[p] for c in coords) + 1 for p in range(3)]
    if math.prod(sizes) != n_slab or len(set(coords)) != n_slab:
        return plain
    axes = []
    for p in range(3):
        unit = tuple(1 if q == p else 0 for q in range(3))
        axes.append((sizes[p], coords.index(unit) if sizes[p] > 1 else 1))
    for index, c in enumerate(coords):
        if any((index // axes[p][1]) % axes[p][0] != c[p] for p in range(3)):
            return plain
    (x, y, z) = axes
    return (z, y, x)


def kernel_body(
    layout, n_kv, scale,
    q_ref, do_ref, o_ref, lse_ref, k_ref, v_ref,
    dq_ref, dk_ref, dv_ref,
    kv, probs, dscores, acc, send_a, recv_a, send_b, recv_b, send_z, recv_z,
    dq_acc, dq_recv, rows,
    gz_s, gz_r, ga_s, ga_r, gb_s, gb_r, ra_s, ra_r, rb_s, rb_r, rz_s, rz_r, kv_s, kv_r,
):
    (nz, sz), (n_first, s_first), (n_second, s_second) = layout
    me = lax.axis_index("slab")
    core = lax.axis_index("kv")
    z = (me // sz) % nz
    first = (me // s_first) % n_first
    second = (me // s_second) % n_second
    na, nb = n_first, n_second
    if na == nb:
        odd = core % 2
        a = first + odd * (second - first)
        b = second + odd * (first - second)
        sa = s_first + odd * (s_second - s_first)
        sb = s_second + odd * (s_first - s_second)
    else:
        a, b, sa, sb = first, second, s_first, s_second
    kb = k_ref.shape[1]
    channels = k_ref.shape[2]
    tokens = q_ref.shape[0]
    col = nz * kb
    started = []

    def zp(d):
        return (z + d) % nz

    def ap(d):
        return (a + d) % na

    def bp(d):
        return (b + d) % nb

    def to_z(d):
        return (me + (zp(d) - z) * sz, core)

    def to_a(d):
        return (me + (ap(d) - a) * sa, core)

    def to_b(d):
        return (me + (bp(d) - b) * sb, core)

    def to_core(d):
        return (me, (core + d) % n_kv)

    def row(block):
        return pl.ds(pl.multiple_of(block * kb, kb), kb)

    def slot(rb, ra, rz):
        return row((bp(nb - rb) * na + ap(na - ra)) * nz + zp(nz - rz))

    def half(rb, rz):
        return row(bp(nb - rb) * nz + zp(nz - rz))

    def remote(src, dst, s, r, device):
        return pltpu.make_async_remote_copy(
            src_ref=src, dst_ref=dst, send_sem=s, recv_sem=r, device_id=device, device_id_type=MESH
        )

    def start(copy):
        copy.start()
        started.append(copy)

    peers = (
        [to_z(d) for d in range(1, nz)]
        + [to_a(d) for d in range(1, na)]
        + [to_b(d) for d in range(1, nb)]
        + [to_core(d) for d in range(1, n_kv)]
    )
    barrier = pltpu.get_barrier_semaphore()
    for peer in peers:
        pl.semaphore_signal(barrier, inc=1, device_id=peer, device_id_type=MESH)
    own = slot(0, 0, 0)
    kv[0, own, :] = k_ref[0]
    kv[1, own, :] = v_ref[0]
    pl.semaphore_wait(barrier, len(peers))

    def block(rb, ra, zb):
        return row((bp(nb - rb) * na + ap(na - ra)) * nz + zb)

    def line_z(way, t, zb):
        s = kv.at[:, block(0, 0, zb), :]
        return remote(s, s, gz_s.at[way, t], gz_r.at[way, t], (me + (1 - 2 * way) * sz, core))

    def gather_a(d, zb):
        s = kv.at[:, block(0, 0, zb), :]
        return remote(s, s, ga_s.at[d - 1, zb], ga_r.at[d - 1, zb], to_a(d))

    def gather_b(d, ra, zb):
        s = kv.at[:, block(0, ra, zb), :]
        return remote(s, s, gb_s.at[d - 1, ra, zb], gb_r.at[d - 1, ra, zb], to_b(d))

    def arrived_a(d, zb):
        s = kv.at[:, block(0, d, zb), :]
        remote(s, s, ga_s.at[d - 1, zb], ga_r.at[d - 1, zb], to_a(d)).wait_recv()

    def arrived_b(d, ra, zb):
        s = kv.at[:, block(d, ra, zb), :]
        remote(s, s, gb_s.at[d - 1, ra, zb], gb_r.at[d - 1, ra, zb], to_b(d)).wait_recv()

    def from_z(way, t):
        zb = z - 1 - t if way == 0 else z + 1 + t
        return zb, (zb >= 0 if way == 0 else zb < nz)

    def has_next(way):
        return z + 1 < nz if way == 0 else z >= 1

    def spread(zb):
        for d in range(1, na):
            gather_a(d, zb).start()
        for d in range(1, nb):
            gather_b(d, 0, zb).start()

    def pass_b(zb):
        for d in range(1, na):
            arrived_a(d, zb)
            for e in range(1, nb):
                gather_b(e, d, zb).start()

    def step_z(t):
        for way in range(2):
            zb, there = from_z(way, t)

            @pl.when(there)
            def _():
                s = kv.at[:, block(0, 0, zb), :]
                remote(
                    s, s, gz_s.at[way, t], gz_r.at[way, t], (me + (2 * way - 1) * sz, core)
                ).wait_recv()
                if t + 1 < nz - 1:
                    @pl.when(has_next(way))
                    def _():
                        line_z(way, t + 1, zb).start()
                spread(zb)

    def step_a(t):
        for way in range(2):
            zb, there = from_z(way, t)

            @pl.when(there)
            def _():
                pass_b(zb)

    if nz > 1:
        for way in range(2):
            @pl.when(has_next(way))
            def _():
                line_z(way, 0, z).start()
    spread(z)

    qt = min(256, tokens)
    log2e = math.log2(math.e)

    @pl.loop(0, tokens // qt)
    def _(t):
        here = pl.ds(pl.multiple_of(t * qt, qt), qt)
        prod = do_ref[here, :].astype(F32) * o_ref[here, :].astype(F32)
        part = prod[:, :128]
        for lane in range(128, channels, 128):
            part = part + prod[:, lane : lane + 128]
        rows[1:2, here] = jnp.sum(part.T, axis=0, keepdims=True)
        rows[0:1, here] = lse_ref[:, here] * log2e

    for t in range(nz - 1):
        step_z(t)
        if t == 0:
            pass_b(z)
        else:
            step_a(t - 1)
    if nz == 1:
        pass_b(z)

    kt = min(256, col)

    def column(rb, ra):
        top = pl.multiple_of((bp(nb - rb) * na + ap(na - ra)) * col, col)
        local = pl.multiple_of(bp(nb - rb) * col, col)

        @pl.loop(0, tokens // qt)
        def _(t):
            here = pl.ds(pl.multiple_of(t * qt, qt), qt)
            contract = (((1,), (1,)), ((), ()))
            span = pl.ds(top, col)
            s = lax.dot_general(kv[0, span, :], q_ref[here, :], contract, preferred_element_type=F32)
            p = jnp.exp2(s * (scale * log2e) - rows[0:1, here])
            dp = lax.dot_general(kv[1, span, :], do_ref[here, :], contract, preferred_element_type=F32)
            probs[:, here] = p.astype(BF16)
            dscores[span, here] = (p * (dp - rows[1:2, here])).astype(BF16)

        @pl.loop(0, col // kt)
        def _(t):
            off = t * kt
            span = pl.ds(pl.multiple_of(top + off, kt), kt)
            dk = jnp.dot(dscores[span, :], q_ref[...], preferred_element_type=F32)
            dv = jnp.dot(
                probs[pl.ds(pl.multiple_of(off, kt), kt), :], do_ref[...], preferred_element_type=F32
            )
            if ra == 0:
                there = pl.ds(pl.multiple_of(local + off, kt), kt)
                acc[0, there, :] = dk
                acc[1, there, :] = dv
            else:
                send_a[0, span, :] = dk.astype(BF16)
                send_a[1, span, :] = dv.astype(BF16)

    order_z = list(range(1, nz)) + [0]

    def reduce_a(ra, rb, rz):
        d = na - ra
        return remote(
            send_a.at[:, slot(rb, ra, rz), :], recv_a.at[d - 1, :, half(rb, rz), :],
            ra_s.at[d - 1, rb, rz], ra_r.at[d - 1, rb, rz], to_a(d),
        )

    def summed_a(d, rb, rz):
        here = half(rb, rz)
        dst = recv_a.at[d - 1, :, here, :]
        remote(dst, dst, ra_s.at[d - 1, rb, rz], ra_r.at[d - 1, rb, rz], to_a(d)).wait_recv()

    def reduce_b(rb, rz):
        d = nb - rb
        return remote(
            send_b.at[:, half(rb, rz), :], recv_b.at[d - 1, :, row(zp(nz - rz)), :],
            rb_s.at[d - 1, rz], rb_r.at[d - 1, rz], to_b(d),
        )

    def summed_b(d, rz):
        dst = recv_b.at[d - 1, :, row(zp(nz - rz)), :]
        remote(dst, dst, rb_s.at[d - 1, rz], rb_r.at[d - 1, rz], to_b(d)).wait_recv()

    def reduce_z(rz):
        d = nz - rz
        return remote(
            send_z.at[:, row(zp(d)), :], recv_z.at[d - 1], rz_s.at[d - 1], rz_r.at[d - 1], to_z(d)
        )

    column(0, 0)
    if nz > 1:
        step_a(nz - 2)
    for ra in range(1, na):
        column(0, ra)
        for rz in order_z:
            start(reduce_a(ra, 0, rz))
    for rb in range(1, nb):
        for zb in range(nz):
            arrived_b(rb, 0, zb)
        column(rb, 0)
    ahead = 2
    for rb in range(1, nb):
        for ra in range(1, na):
            for zb in range(nz):
                arrived_b(rb, ra, zb)
            column(rb, ra)
            for rz in order_z[:ahead]:
                start(reduce_a(ra, rb, rz))

    width = channels // n_kv

    @pl.loop(0, tokens // qt)
    def _(t):
        here = pl.ds(pl.multiple_of(t * qt, qt), qt)
        dq = lax.dot_general(
            dscores[:, here], kv[0], (((0,), (0,)), ((), ())), preferred_element_type=F32
        )
        for c in range(n_kv):
            dq_acc[c, here, :] = dq[:, c * width : (c + 1) * width]

    for d in range(1, n_kv):
        start(remote(
            dq_acc.at[(core + d) % n_kv], dq_recv.at[d - 1], kv_s.at[d - 1], kv_r.at[d - 1], to_core(d)
        ))

    def sum_a(rb, rz):
        here = half(rb, rz)
        total = acc[:, here, :]
        for d in range(1, na):
            summed_a(d, rb, rz)
            total = total + recv_a[d - 1, :, here, :].astype(F32)
        return total

    def finish(rz):
        total = sum_a(0, rz)
        for d in range(1, nb):
            summed_b(d, rz)
            total = total + recv_b[d - 1, :, row(zp(nz - rz)), :].astype(F32)
        if rz != 0:
            send_z[:, row(zp(nz - rz)), :] = total.astype(BF16)
            start(reduce_z(rz))
        else:
            acc[:, half(0, 0), :] = total

    for k, rz in enumerate(order_z):
        for rb in range(1, nb):
            total = sum_a(rb, rz)
            if k + ahead < nz:
                for ra in range(1, na):
                    start(reduce_a(ra, rb, order_z[k + ahead]))
            send_b[:, half(rb, rz), :] = total.astype(BF16)
            start(reduce_b(rb, rz))
        if k > 0:
            finish(order_z[k - 1])
    finish(order_z[-1])

    for d in range(1, n_kv):
        dst = dq_recv.at[d - 1]
        remote(dst, dst, kv_s.at[d - 1], kv_r.at[d - 1], to_core(d)).wait_recv()
    dq = dq_acc[core]
    for d in range(1, n_kv):
        dq = dq + dq_recv[d - 1]
    dq_ref[...] = (dq * scale).astype(BF16)

    total = acc[:, half(0, 0), :]
    for d in range(1, nz):
        dst = recv_z.at[d - 1]
        remote(dst, dst, rz_s.at[d - 1], rz_r.at[d - 1], to_z(d)).wait_recv()
        total = total + recv_z[d - 1].astype(F32)
    dk_ref[0] = (total[0] * scale).astype(BF16)
    dv_ref[0] = total[1].astype(BF16)
    for copy in started:
        copy.wait_send()
    for zb in range(nz):
        for d in range(1, na):
            gather_a(d, zb).wait_send()
        for d in range(1, nb):
            for ra in range(na):
                gather_b(d, ra, zb).wait_send()
    for t in range(nz - 1):
        for way in range(2):
            zb = z - t if way == 0 else z + t
            held = jnp.logical_and(has_next(way), zb >= 0 if way == 0 else zb < nz)

            @pl.when(held)
            def _():
                line_z(way, t, zb).wait_send()


def solution(mesh):
    layout = slab_layout(mesh)
    n_kv = mesh.shape["kv"]
    (nz, _), (na, _), (nb, _) = layout

    def on_device(queries, grad_out, attn_out, row_lse, keys, values):
        tokens, channels = queries.shape
        kb = keys.shape[1]
        scale = channels ** (-0.5)
        col = nz * kb
        panel = na * nb * col
        width = channels // n_kv
        dma = pltpu.SemaphoreType.DMA

        def sems(*dims):
            dims = tuple(max(d, 1) for d in dims)
            return [dma(dims), dma(dims)]

        def buf(dtype, *dims):
            return pltpu.VMEM(tuple(max(d, 1) for d in dims), dtype)

        vmem = pl.BlockSpec(memory_space=pltpu.VMEM)
        return pl.pallas_call(
            functools.partial(kernel_body, layout, n_kv, scale),
            out_shape=(
                jax.ShapeDtypeStruct((tokens, width), BF16),
                jax.ShapeDtypeStruct(keys.shape, BF16),
                jax.ShapeDtypeStruct(values.shape, BF16),
            ),
            in_specs=[vmem] * 6,
            out_specs=(vmem,) * 3,
            scratch_shapes=[
                buf(BF16, 2, panel, channels),
                buf(BF16, col, tokens),
                buf(BF16, panel, tokens),
                buf(F32, 2, nb * col, channels),
                buf(BF16, 2, panel, channels),
                buf(BF16, na - 1, 2, nb * col, channels),
                buf(BF16, 2, nb * col, channels),
                buf(BF16, nb - 1, 2, col, channels),
                buf(BF16, 2, col, channels),
                buf(BF16, nz - 1, 2, kb, channels),
                buf(F32, n_kv, tokens, width),
                buf(F32, n_kv - 1, tokens, width),
                buf(F32, 8, tokens),
                *sems(2, nz - 1),
                *sems(na - 1, nz),
                *sems(nb - 1, na, nz),
                *sems(na - 1, nb, nz),
                *sems(nb - 1, nz),
                *sems(nz - 1),
                *sems(n_kv - 1),
            ],
            compiler_params=pltpu.CompilerParams(
                collective_id=0, has_side_effects=True, vmem_limit_bytes=56 * 1024 * 1024
            ),
            name="attention_backward",
        )(queries, grad_out, attn_out, row_lse.reshape(1, tokens), keys, values)

    placed = (
        P("slab", None),
        P("slab", None),
        P("slab", None),
        P("slab"),
        P("kv", "slab", None),
        P("kv", "slab", None),
    )
    return jax.shard_map(
        on_device,
        mesh=mesh,
        in_specs=placed,
        out_specs=(P("slab", "kv"), P("kv", "slab", None), P("kv", "slab", None)),
        check_vma=False,
    )
```
